32 devices in a mesh: grp: 2 (over y), sp: 4 (over z), tm: 2 (over x), mdl: 2 (over core).
Axes of the slice: x: 2, y: 2, z: 4, core: 2. Of those that a mesh axis runs over, the one named last changes fastest.
Arguments:
- features: bfloat16 [2, 16, 128, 128, 128], P('grp', 'tm', 'mdl', 'sp'), parts along dimension 0, may hold values from -32 to 32
- conv_kernel: bfloat16 [3, 3, 3, 12, 128], P(None, None, None, None, 'mdl'), may hold values from -0.109375 to 0.109375
- patch_weight: bfloat16 [768, 1024], replicated, may hold values from -0.21875 to 0.21875
- position_table: bfloat16 [256, 1024], replicated, may hold values from -6 to 6
- gain_one: float32 [1024], replicated, may hold values from 0.1 to 1.9
- query_weight: bfloat16 [1024, 1024], P('sp'), may hold values from -1 to 1
- key_weight: bfloat16 [1024, 1024], P('sp'), may hold values from -1 to 1
- value_weight: bfloat16 [1024, 1024], P('sp'), may hold values from -0.1875 to 0.1875
- out_weight: bfloat16 [1024, 1024], P('sp'), may hold values from -0.1875 to 0.1875
- gain_two: float32 [1024], replicated, may hold values from 0.1 to 1.9
- head_vector: float32 [1024], replicated, may hold values from -6 to 6
- frame_weight: float32 [8, 2, 2], P(('grp', 'sp'), 'tm', 'mdl'), parts along dimension 0, may hold values from 0.5 to 1.5
Outputs:
- rewards: float32 [8, 2, 2], P(('grp', 'sp'), 'tm', 'mdl'), parts along dimension 0
- feature_grad: bfloat16 [2, 16, 128, 128, 128], P('grp', 'tm', 'mdl', 'sp'), parts along dimension 0
The draws below stay inside these ranges and needn't reach their ends.
There are 2 independent parts, one for each index of `grp`. The reference program is written for one: setup_inputs(seed, part) draws one part's arguments, and reference() takes and returns one part's arrays. A program takes and returns all parts, laid end to end along the dimension named above; an argument that names none is the same for every part. Nothing has to cross between parts.
All inputs are finite; a program needn't handle non-finite values.
Results may differ from the reference program's by a relative error of at most 0.035.
Values may be sent and summed in bfloat16 or wider, within the bound.
A program may use at most 448 MiB of HBM per device.

```python
import math
import jax
import jax.numpy as jnp
from jax import lax

D = 1024
HEADS = 16
HEAD_DIM = 64
PATCH = 16
PIX = 768
IMG = 256
HH = 128
TOKENS_F = 256
FRAMES = 16
FD = 8
CLIPS = 1
CHAN = 128
N_SP = 4
N_TM = 2
N_MDL = 2


def draw_query_weight(key, part):
    key = jax.random.fold_in(key, 1)
    return (jnp.clip(jax.random.normal(key, (D, D), jnp.float32), -4.0, 4.0) / math.sqrt(D)).astype(jnp.bfloat16)


def draw_key_weight(key, part):
    key = jax.random.fold_in(key, 2)
    jitter = jnp.clip(jax.random.normal(key, (D, D), jnp.float32), -4.0, 4.0) / math.sqrt(D)
    return jitter.astype(jnp.bfloat16)


def draw_features(key, part):
    key = jax.random.fold_in(key, 3)
    shape = (CLIPS, FRAMES, CHAN, HH, HH)
    row_scale = jnp.exp(jax.random.uniform(jax.random.fold_in(key, 1), (CLIPS, FRAMES, 1, HH, 1), jnp.float32, math.log(0.4), math.log(4.0)))
    channel_scale = jnp.exp(jax.random.uniform(jax.random.fold_in(key, 2), (1, 1, CHAN, 1, 1), jnp.float32, math.log(0.5), math.log(2.0)))
    base = jnp.clip(jax.random.normal(jax.random.fold_in(key, 4), shape, jnp.float32), -4.0, 4.0)
    return (base * row_scale * channel_scale).astype(jnp.bfloat16)


def block_scale(key, extent, cuts, low, top_value):
    factor_of, own = 1.0, jax.random.fold_in(key, 6)
    for position, blocks in cuts:
        draws = jnp.exp(jax.random.uniform(jax.random.fold_in(own, position), (blocks,), jnp.float32, low / len(cuts), top_value / len(cuts)))
        factor_of = factor_of * jnp.repeat(draws, extent[position] // blocks).reshape([-1 if axis == position else 1 for axis in range(len(extent))])
    return factor_of


def bell_draw(own_key, extent, width, limit, pieces=(), held_as=jnp.bfloat16):
    level = block_scale(own_key, extent, pieces, -0.22, 0.18) if pieces else 1.0
    drawn = jax.random.normal(own_key, extent, jnp.float32) * width * level
    return jnp.minimum(jnp.maximum(drawn, -limit), limit).astype(held_as)


def setup_inputs(seed: int = 0, part: int = 0) -> dict:
    arg_keys = jax.random.split(jax.random.key(seed), 13)
    part_keys = jax.random.split(jax.random.fold_in(arg_keys[12], part), 13)
    features = draw_features(jax.random.fold_in(jax.random.fold_in(arg_keys[12], part), 71), part)
    conv_kernel = bell_draw(arg_keys[1], (3, 3, 3, 12, CHAN), (27 * CHAN) ** -0.5, 0.109375, ((4, 2),))
    patch_weight = bell_draw(arg_keys[2], (PIX, D), PIX ** -0.5, 0.21875)
    position_table = bell_draw(arg_keys[3], (TOKENS_F, D), 1.0, 6.0)
    gain_one = jnp.clip(1.0 + 0.18 * jax.random.normal(arg_keys[4], (D,), jnp.float32), 0.1, 1.9)
    query_weight = draw_query_weight(jax.random.fold_in(arg_keys[12], 71), part)
    key_weight = draw_key_weight(jax.random.fold_in(arg_keys[12], 71), part)
    value_weight = bell_draw(arg_keys[7], (D, D), D ** -0.5, 0.1875, ((0, 4),))
    out_weight = bell_draw(arg_keys[8], (D, D), D ** -0.5, 0.1875, ((0, 4),))
    gain_two = jnp.clip(1.0 + 0.18 * jax.random.normal(arg_keys[9], (D,), jnp.float32), 0.1, 1.9)
    head_vector = bell_draw(arg_keys[10], (D,), 1.0, 6.0, (), jnp.float32)
    frame_weight = jnp.clip(0.5 + 1.0 * jax.random.uniform(part_keys[11], (N_SP, N_TM, N_MDL), jnp.float32) ** block_scale(part_keys[11], (N_SP, N_TM, N_MDL), ((0, 4), (1, 2), (2, 2)), -0.2, 0.2), 0.5, 1.5)
    return {"features": features, "conv_kernel": conv_kernel, "patch_weight": patch_weight, "position_table": position_table, "gain_one": gain_one, "query_weight": query_weight, "key_weight": key_weight, "value_weight": value_weight, "out_weight": out_weight, "gain_two": gain_two, "head_vector": head_vector, "frame_weight": frame_weight}


loss_scale = 1024.0
norm_eps = 1e-05

def silu_slope(values):
    logistic = jax.nn.sigmoid(values)
    return logistic * (1.0 + values * (1.0 - logistic))

def layer_norm(values, gain):
    center = values - lax.optimization_barrier(jnp.mean(values, axis=-1, keepdims=True))
    inverse = lax.rsqrt(lax.optimization_barrier(jnp.mean(center * center, axis=-1, keepdims=True)) + norm_eps)
    normed = center * inverse
    return (normed * gain, normed, inverse)

def norm_back(upstream, normed, inverse, gain):
    scaled = upstream * gain
    return inverse * (scaled - lax.optimization_barrier(jnp.mean(scaled, axis=-1, keepdims=True)) - normed * lax.optimization_barrier(jnp.mean(scaled * normed, axis=-1, keepdims=True)))

def to_pixels(colors):
    lead = colors.shape[:-3]
    rows_in = colors.shape[-2]
    cols_in = colors.shape[-1]
    split = colors.reshape(lead + (3, 2, 2, rows_in, cols_in))
    moved = jnp.moveaxis(split, (-5, -4, -3, -2, -1), (-5, -3, -1, -4, -2))
    return moved.reshape(lead + (3, 2 * rows_in, 2 * cols_in))

def from_pixels(pixels):
    lead = pixels.shape[:-3]
    rows_in = pixels.shape[-2] // 2
    cols_in = pixels.shape[-1] // 2
    split = pixels.reshape(lead + (3, rows_in, 2, cols_in, 2))
    moved = jnp.moveaxis(split, (-5, -4, -3, -2, -1), (-5, -2, -4, -1, -3))
    return moved.reshape(lead + (12, rows_in, cols_in))

def reward_pass(pixels, weight, patch_weight, position_table, gain_one, query_weight, key_weight, value_weight, out_weight, gain_two, head_vector):
    f32 = jnp.float32
    bf16 = jnp.bfloat16
    patch_count = IMG // PATCH
    patches = pixels.reshape(3, patch_count, PATCH, patch_count, PATCH).transpose(1, 3, 0, 2, 4).reshape(TOKENS_F, PIX)
    tokens = (jnp.dot(patches, patch_weight, preferred_element_type=f32) + position_table.astype(f32)).astype(bf16)
    normed_one, unit_one, inverse_one = layer_norm(tokens.astype(f32), gain_one)
    hidden = normed_one.astype(bf16)
    queries = jnp.dot(hidden, query_weight, preferred_element_type=f32).astype(bf16).reshape(TOKENS_F, HEADS, HEAD_DIM)
    key_rows = jnp.dot(hidden, key_weight, preferred_element_type=f32).astype(bf16).reshape(TOKENS_F, HEADS, HEAD_DIM)
    value_rows = jnp.dot(hidden, value_weight, preferred_element_type=f32).astype(bf16).reshape(TOKENS_F, HEADS, HEAD_DIM)
    factor = 1.0 / math.sqrt(HEAD_DIM)
    scores = jnp.einsum('thd,shd->hts', queries.astype(f32), key_rows.astype(f32)) * factor
    attention = jax.nn.softmax(scores, axis=-1)
    attention_low = attention.astype(bf16)
    mixture = jnp.einsum('hts,shd->thd', attention_low.astype(f32), value_rows.astype(f32)).astype(bf16).reshape(TOKENS_F, D)
    stream = tokens.astype(f32) + jnp.dot(mixture, out_weight, preferred_element_type=f32)
    normed_two, unit_two, inverse_two = layer_norm(stream, gain_two)
    reward = jnp.sum(normed_two * head_vector) / TOKENS_F
    upstream = jnp.broadcast_to(head_vector * (loss_scale * weight / TOKENS_F), (TOKENS_F, D))
    grad_stream = norm_back(upstream, unit_two, inverse_two, gain_two)
    grad_mixture = jnp.dot(grad_stream.astype(bf16), out_weight.T, preferred_element_type=f32).astype(bf16).reshape(TOKENS_F, HEADS, HEAD_DIM)
    grad_attention = jnp.einsum('thd,shd->hts', grad_mixture.astype(f32), value_rows.astype(f32))
    grad_scores = (attention * (grad_attention - lax.optimization_barrier(jnp.sum(attention * grad_attention, axis=-1, keepdims=True))) * factor).astype(bf16)
    grad_queries = jnp.einsum('hts,shd->thd', grad_scores.astype(f32), key_rows.astype(f32)).astype(bf16).reshape(TOKENS_F, D)
    grad_keys = jnp.einsum('hts,thd->shd', grad_scores.astype(f32), queries.astype(f32)).astype(bf16).reshape(TOKENS_F, D)
    grad_values = jnp.einsum('hts,thd->shd', attention_low.astype(f32), grad_mixture.astype(f32)).astype(bf16).reshape(TOKENS_F, D)
    grad_hidden = jnp.dot(grad_queries, query_weight.T, preferred_element_type=f32)
    grad_hidden = grad_hidden + jnp.dot(grad_keys, key_weight.T, preferred_element_type=f32)
    grad_hidden = grad_hidden + jnp.dot(grad_values, value_weight.T, preferred_element_type=f32)
    grad_tokens = (grad_stream + norm_back(grad_hidden, unit_one, inverse_one, gain_one)).astype(bf16)
    grad_patches = jnp.dot(grad_tokens, patch_weight.T, preferred_element_type=f32).astype(bf16)
    grad_pixels = grad_patches.reshape(patch_count, patch_count, 3, PATCH, PATCH).transpose(2, 0, 3, 1, 4).reshape(3, IMG, IMG)
    return (reward, grad_pixels)

def frames_order(values):
    return jnp.transpose(values, (1, 0, 2)).reshape(N_TM, FD, CLIPS).transpose(2, 0, 1).reshape(CLIPS * FRAMES)

def device_order(values):
    return values.reshape(CLIPS, N_TM, FD).transpose(1, 2, 0).reshape(N_TM, N_SP, N_MDL).transpose(1, 0, 2)

def reference(features, conv_kernel, patch_weight, position_table, gain_one, query_weight, key_weight, value_weight, out_weight, gain_two, head_vector, frame_weight):
    f32 = jnp.float32
    bf16 = jnp.bfloat16
    kernel_wide = conv_kernel.astype(f32)

    def clip_forward(clip_features):
        activated = jax.nn.silu(clip_features.astype(f32)).astype(bf16)
        padded = jnp.pad(activated, ((1, 1), (0, 0), (1, 1), (1, 1))).astype(f32)
        colors = jnp.zeros((FRAMES, 12, HH, HH), f32)
        for time_tap in range(3):
            for row_tap in range(3):
                for col_tap in range(3):
                    window_cells = padded[time_tap:time_tap + FRAMES, :, row_tap:row_tap + HH, col_tap:col_tap + HH]
                    colors = colors + jnp.einsum('oc,fcrw->forw', kernel_wide[time_tap, row_tap, col_tap], window_cells)
        return colors.astype(bf16)
    colors = lax.map(clip_forward, features)
    pixels = to_pixels(colors).reshape(CLIPS * FRAMES, 3, IMG, IMG)
    weights_flat = frames_order(frame_weight)

    def score_frame(pair):
        return reward_pass(pair[0], pair[1], patch_weight, position_table, gain_one, query_weight, key_weight, value_weight, out_weight, gain_two, head_vector)
    rewards_flat, grad_pixels = lax.map(score_frame, (pixels, weights_flat))
    grad_colors = from_pixels(grad_pixels.reshape(CLIPS, FRAMES, 3, IMG, IMG))

    def clip_backward(pair):
        grad_clip, clip_features = pair
        padded = jnp.pad(grad_clip, ((1, 1), (0, 0), (1, 1), (1, 1))).astype(f32)
        grad_act = jnp.zeros((FRAMES, CHAN, HH, HH), f32)
        for time_tap in range(3):
            for row_tap in range(3):
                for col_tap in range(3):
                    window_cells = padded[2 - time_tap:2 - time_tap + FRAMES, :, 2 - row_tap:2 - row_tap + HH, 2 - col_tap:2 - col_tap + HH]
                    grad_act = grad_act + jnp.einsum('oc,forw->fcrw', kernel_wide[time_tap, row_tap, col_tap], window_cells)
        return (grad_act * silu_slope(clip_features.astype(f32))).astype(bf16)
    feature_grad = lax.map(clip_backward, (grad_colors, features))
    return (device_order(rewards_flat), feature_grad)
```

```python
import math

import jax
import jax.numpy as jnp
import numpy as np
from jax import lax
from jax.experimental import pallas as pl
from jax.experimental.pallas import tpu as pltpu
from jax.sharding import PartitionSpec as P

D = 1024
HEADS = 16
HEAD_DIM = 64
PATCH = 16
PIX = 768
IMG = 256
TOKENS_F = 256
COLORS = 12
SIDE = IMG // PATCH
HALF = PATCH // 2
VMEM_LIMIT = 56 * 1024 * 1024

loss_scale = 1024.0
norm_eps = 1e-05
f32 = jnp.float32
bf16 = jnp.bfloat16


def sizes(row_count):
    block = min(16, row_count)
    rimmed = -(-(block + 2) // 8) * 8
    deep = 3 * COLORS * rimmed
    padded = -(-deep // 128) * 128
    return block, row_count // block, rimmed, deep, padded


def band_kernel(block, rimmed, conv_ref, fwd_ref, back_ref, spread_ref, wide_ref):
    chans = conv_ref.shape[-1]
    wide = chans * block
    deep = 3 * COLORS * rimmed
    padded = wide_ref.shape[0]
    lane_chan = lax.broadcasted_iota(jnp.int32, (chans, wide), 1) // block
    own_chan = lax.broadcasted_iota(jnp.int32, (chans, wide), 0)
    repeat = jnp.where(lane_chan == own_chan, 1.0, 0.0).astype(bf16)
    lane_row = lax.broadcasted_iota(jnp.int32, (rimmed, wide), 1) % block
    rim_row = lax.broadcasted_iota(jnp.int32, (rimmed, wide), 0)
    masks = [rim_row == lane_row + (2 - tap) for tap in range(3)]
    for col_tap in range(3):
        for row_tap in range(3):
            spread_ref[row_tap] = jnp.dot(
                conv_ref[row_tap, col_tap], repeat, preferred_element_type=f32
            )

        @pl.loop(0, 3 * COLORS)
        def _(line):
            total = jnp.zeros((rimmed, wide), f32)
            for row_tap in range(3):
                row = spread_ref[row_tap, pl.ds(line, 1), :]
                total = jnp.where(masks[row_tap], jnp.broadcast_to(row, (rimmed, wide)), total)
            wide_ref[pl.ds(pl.multiple_of(line * rimmed, 8), rimmed), :] = total

        if padded > deep:
            wide_ref[deep:, :] = jnp.zeros((padded - deep, wide), f32)
        fwd_ref[:, col_tap * wide : (col_tap + 1) * wide] = wide_ref[...].astype(bf16)
        back_ref[:, col_tap * padded : (col_tap + 1) * padded] = wide_ref[...].T.astype(bf16)


def band_matrices(conv_kernel, row_count):
    block, _, rimmed, deep, padded = sizes(row_count)
    chans = conv_kernel.shape[-1]
    wide = chans * block
    taps = conv_kernel.transpose(1, 2, 0, 3, 4).reshape(3, 3, 3 * COLORS, chans)

    def body(*refs):
        band_kernel(block, rimmed, *refs)

    return pl.pallas_call(
        body,
        out_shape=(
            jax.ShapeDtypeStruct((padded, 3 * wide), bf16),
            jax.ShapeDtypeStruct((wide, 3 * padded), bf16),
        ),
        in_specs=[pl.BlockSpec(memory_space=pltpu.VMEM)],
        out_specs=(pl.BlockSpec(memory_space=pltpu.VMEM), pl.BlockSpec(memory_space=pltpu.VMEM)),
        scratch_shapes=[pltpu.VMEM((3, 3 * COLORS, wide), f32), pltpu.VMEM((padded, wide), f32)],
        compiler_params=pltpu.CompilerParams(vmem_limit_bytes=VMEM_LIMIT),
        name="band_matrices",
    )(taps)


def column_shifts(values):
    width = values.shape[-1]
    lane = lax.broadcasted_iota(jnp.int32, values.shape, values.ndim - 1)
    before = jnp.where(lane == 0, 0.0, pltpu.roll(values, 1, axis=values.ndim - 1))
    after = jnp.where(lane == width - 1, 0.0, pltpu.roll(values, width - 1, axis=values.ndim - 1))
    return before, values, after


def color_kernel(dims, features_ref, band_ref, main_ref, total_ref, cells_ref):
    frame_count, row_count, block, blocks, rimmed, deep = dims
    chans, width = features_ref.shape[2], features_ref.shape[4]
    wide = chans * block
    total_ref[...] = jnp.zeros_like(total_ref)
    for first in range(0, frame_count, 2):
        for band in range(blocks):
            for half in range(2):
                raw = features_ref[0, first + half, :, band * block : (band + 1) * block, :]
                values = raw.astype(f32).reshape(wide, width)
                active = (values / (1.0 + jnp.exp(-values))).astype(bf16).astype(f32)
                for col_tap, shifted in enumerate(column_shifts(active)):
                    cells_ref[
                        col_tap * wide : (col_tap + 1) * wide, half * width : (half + 1) * width
                    ] = shifted.astype(bf16)
            product = jnp.dot(band_ref[...], cells_ref[...], preferred_element_type=f32)
            product = product[:deep].reshape(3, COLORS, rimmed, 2 * width)
            for half in range(2):
                for time_tap in range(3):
                    total_ref[
                        first + half - time_tap + 2, :, band * block : band * block + rimmed, :
                    ] += product[time_tap, :, :, half * width : (half + 1) * width]
    rows = COLORS * row_count
    for frame in range(frame_count + 2):
        part = total_ref[frame]
        main_ref[frame, 0, 0:rows, :] = (
            part[:, 1 : row_count + 1, :].reshape(rows, width).astype(bf16)
        )
        spare = jnp.zeros((4, width), f32)
        top = [part[color, 0:1, :] for color in range(COLORS)]
        low = [part[color, row_count + 1 : row_count + 2, :] for color in range(COLORS)]
        main_ref[frame, 0, rows:, :] = jnp.concatenate(top + [spare] + low + [spare]).astype(bf16)


def partial_colors(features, band):
    clip_count, frame_count, chans, row_count, width = features.shape
    block, blocks, rimmed, deep, padded = sizes(row_count)
    rows = COLORS * row_count + 32
    stored = (blocks - 1) * block + rimmed
    dims = (frame_count, row_count, block, blocks, rimmed, deep)

    def body(*refs):
        color_kernel(dims, *refs)

    return pl.pallas_call(
        body,
        grid=(clip_count,),
        out_shape=jax.ShapeDtypeStruct((frame_count + 2, clip_count, rows, width), bf16),
        in_specs=[
            pl.BlockSpec((1, frame_count, chans, row_count, width), lambda clip: (clip, 0, 0, 0, 0)),
            pl.BlockSpec(memory_space=pltpu.VMEM),
        ],
        out_specs=pl.BlockSpec((frame_count + 2, 1, rows, width), lambda clip: (0, clip, 0, 0)),
        scratch_shapes=[
            pltpu.VMEM((frame_count + 2, COLORS, stored, width), f32),
            pltpu.VMEM((3 * chans * block, 2 * width), bf16),
        ],
        compiler_params=pltpu.CompilerParams(vmem_limit_bytes=VMEM_LIMIT),
        name="partial_colors",
    )(features, band)


def color_backward_kernel(dims, grad_ref, features_ref, band_ref, out_ref, rim_ref, shift_ref, cells_ref):
    frame_count, row_count, block, blocks, rimmed, deep, padded = dims
    chans, width = features_ref.shape[2], features_ref.shape[4]
    rows = COLORS * row_count
    color_rows = COLORS * rimmed
    stored = rim_ref.shape[1]
    for frame in range(frame_count + 2):
        for color in range(COLORS):
            rim_ref[color, 1 : row_count + 1, :] = grad_ref[
                frame, 0, color * row_count : (color + 1) * row_count, :
            ].astype(f32)
        edges = grad_ref[frame, 0, rows:, :].astype(f32)
        for color in range(COLORS):
            rim_ref[color, 0:1, :] = edges[color : color + 1]
            rim_ref[color, row_count + 1 : row_count + 2, :] = edges[16 + color : 17 + color]
            rim_ref[color, row_count + 2 :, :] = jnp.zeros((stored - row_count - 2, width), f32)
        for band in range(blocks):
            lines = rim_ref[:, band * block : band * block + rimmed, :].reshape(color_rows, width)
            before, same, after = column_shifts(lines)
            for col_tap, shifted in enumerate((after, same, before)):
                shift_ref[col_tap, frame, band] = shifted.astype(bf16)
    if padded > deep:
        for col_tap in range(3):
            cells_ref[col_tap * padded + deep : (col_tap + 1) * padded, :] = jnp.zeros(
                (padded - deep, 2 * width), bf16
            )
    for first in range(0, frame_count, 2):
        for band in range(blocks):
            for half in range(2):
                for col_tap in range(3):
                    for time_tap in range(3):
                        begin = col_tap * padded + time_tap * color_rows
                        cells_ref[
                            begin : begin + color_rows, half * width : (half + 1) * width
                        ] = shift_ref[col_tap, first + half - time_tap + 2, band]
            product = jnp.dot(band_ref[...], cells_ref[...], preferred_element_type=f32)
            for half in range(2):
                values = features_ref[
                    0, first + half, :, band * block : (band + 1) * block, :
                ].astype(f32)
                logistic = 1.0 / (1.0 + jnp.exp(-values))
                slope = logistic * (1.0 + values * (1.0 - logistic))
                grad = product[:, half * width : (half + 1) * width].reshape(chans, block, width)
                out_ref[0, first + half, :, band * block : (band + 1) * block, :] = (
                    grad * slope
                ).astype(bf16)


def color_backward(grads, features, band):
    clip_count, frame_count, chans, row_count, width = features.shape
    block, blocks, rimmed, deep, padded = sizes(row_count)
    rows = COLORS * row_count + 32
    stored = (blocks - 1) * block + rimmed
    dims = (frame_count, row_count, block, blocks, rimmed, deep, padded)
    whole = pl.BlockSpec((1, frame_count, chans, row_count, width), lambda clip: (clip, 0, 0, 0, 0))

    def body(*refs):
        color_backward_kernel(dims, *refs)

    return pl.pallas_call(
        body,
        grid=(clip_count,),
        out_shape=jax.ShapeDtypeStruct(features.shape, bf16),
        in_specs=[
            pl.BlockSpec((frame_count + 2, 1, rows, width), lambda clip: (0, clip, 0, 0)),
            whole,
            pl.BlockSpec(memory_space=pltpu.VMEM),
        ],
        out_specs=whole,
        scratch_shapes=[
            pltpu.VMEM((COLORS, stored, width), f32),
            pltpu.VMEM((3, frame_count + 2, blocks, COLORS * rimmed, width), bf16),
            pltpu.VMEM((3 * padded, 2 * width), bf16),
        ],
        compiler_params=pltpu.CompilerParams(vmem_limit_bytes=VMEM_LIMIT),
        name="color_backward",
    )(grads, features, band)


def patch_order():
    table = np.zeros((HALF, 128, PIX), np.float32)
    for color in range(COLORS):
        k, a, b = color // 4, (color // 2) % 2, color % 2
        for i in range(HALF):
            for j in range(HALF):
                table[j, color * HALF + i, k * PATCH * PATCH + (2 * i + a) * PATCH + 2 * j + b] = 1
    return jnp.asarray(table.reshape(HALF * 128, PIX), bf16)


def layer_norm(values, gain):
    center = values - jnp.mean(values, axis=-1, keepdims=True)
    inverse = lax.rsqrt(jnp.mean(center * center, axis=-1, keepdims=True) + norm_eps)
    normed = center * inverse
    return (normed * gain, normed, inverse)


def norm_back(upstream, normed, inverse, gain):
    scaled = upstream * gain
    return inverse * (
        scaled
        - jnp.mean(scaled, axis=-1, keepdims=True)
        - normed * jnp.mean(scaled * normed, axis=-1, keepdims=True)
    )


def dot(left, right):
    return jnp.dot(left, right, preferred_element_type=f32)


def dot_t(left, right):
    return lax.dot_general(left, right, (((1,), (1,)), ((), ())), preferred_element_type=f32)


def t_dot(left, right):
    return lax.dot_general(left, right, (((0,), (0,)), ((), ())), preferred_element_type=f32)


def reward_kernel(
    parts_ref,
    weight_ref,
    order_ref,
    patch_ref,
    position_ref,
    gain_one_ref,
    query_ref,
    key_ref,
    value_ref,
    out_ref,
    gain_two_ref,
    head_ref,
    reward_ref,
    grad_ref,
    colors_ref,
    turned_ref,
    tokens_ref,
    q_ref,
    k_ref,
    v_ref,
    gm_ref,
    mix_ref,
    gq_ref,
    gk_ref,
    gv_ref,
    att_ref,
):
    bands, cores = parts_ref.shape[0], parts_ref.shape[1]
    width = parts_ref.shape[-1]
    row_count = width // bands
    rows = COLORS * row_count
    edges = []
    for band in range(bands):
        part = parts_ref[band, 0].astype(f32)
        for core in range(1, cores):
            part = part + parts_ref[band, core].astype(f32)
        for color in range(COLORS):
            colors_ref[color, band * row_count : (band + 1) * row_count, :] = part[
                color * row_count : (color + 1) * row_count
            ]
        edges.append(part[rows:])
    for band in range(bands):
        for color in range(COLORS):
            if band > 0:
                at = band * row_count - 1
                colors_ref[color, at : at + 1, :] += edges[band][color : color + 1]
            if band < bands - 1:
                at = (band + 1) * row_count
                colors_ref[color, at : at + 1, :] += edges[band][16 + color : 17 + color]
    spare = jnp.zeros((128 - COLORS * HALF, width), f32)
    for p in range(SIDE):
        lines = [colors_ref[color, p * HALF : (p + 1) * HALF, :] for color in range(COLORS)]
        turned_ref[p] = jnp.concatenate(lines + [spare]).T
    for p in range(SIDE):
        for j in range(HALF):
            tokens_ref[p * SIDE : (p + 1) * SIDE, j * 128 : (j + 1) * 128] = turned_ref[
                p, pl.ds(j, SIDE, stride=HALF), :
            ].astype(bf16)
    patches = dot(tokens_ref[...], order_ref[...]).astype(bf16)
    tokens = (dot(patches, patch_ref[...]) + position_ref[...].astype(f32)).astype(bf16)
    gain_one = gain_one_ref[...]
    gain_two = gain_two_ref[...]
    head = head_ref[...]
    normed_one, unit_one, inverse_one = layer_norm(tokens.astype(f32), gain_one)
    hidden = normed_one.astype(bf16)
    q_ref[...] = dot(hidden, query_ref[...]).astype(bf16)
    k_ref[...] = dot(hidden, key_ref[...]).astype(bf16)
    v_ref[...] = dot(hidden, value_ref[...]).astype(bf16)
    factor = 1.0 / math.sqrt(HEAD_DIM)
    pair_width = 2 * HEAD_DIM
    side = lax.broadcasted_iota(jnp.int32, (TOKENS_F, pair_width), 1) // HEAD_DIM
    zero = jnp.zeros((TOKENS_F, pair_width), bf16)

    def split(values):
        return [jnp.where(side == half, values, zero) for half in range(2)]

    for pair in range(HEADS // 2):
        span = slice(pair * pair_width, (pair + 1) * pair_width)
        queries = split(q_ref[:, span])
        keys = k_ref[:, span]
        low = []
        for half in range(2):
            scores = dot_t(queries[half], keys) * factor
            powers = jnp.exp(scores - jnp.max(scores, axis=-1, keepdims=True))
            attention = powers * (1.0 / jnp.sum(powers, axis=-1, keepdims=True))
            att_ref[2 * pair + half] = attention
            low.append(attention.astype(bf16))
        values = split(v_ref[:, span])
        mix_ref[:, span] = dot(
            jnp.concatenate(low, axis=1), jnp.concatenate(values, axis=0)
        ).astype(bf16)
    stream = tokens.astype(f32) + dot(mix_ref[...], out_ref[...])
    normed_two, unit_two, inverse_two = layer_norm(stream, gain_two)
    reward_ref[...] = (
        jnp.sum(jnp.sum(normed_two * head, axis=0, keepdims=True), axis=1, keepdims=True) / TOKENS_F
    )
    upstream = head * (loss_scale * weight_ref[...] / TOKENS_F)
    grad_stream = norm_back(upstream, unit_two, inverse_two, gain_two)
    gm_ref[...] = dot_t(grad_stream.astype(bf16), out_ref[...]).astype(bf16)
    for pair in range(HEADS // 2):
        span = slice(pair * pair_width, (pair + 1) * pair_width)
        upper = split(gm_ref[:, span])
        values = v_ref[:, span]
        slopes, low = [], []
        for half in range(2):
            attention = att_ref[2 * pair + half]
            grad_attention = dot_t(upper[half], values)
            weighted = attention * grad_attention
            slopes.append(
                (
                    (weighted - attention * jnp.sum(weighted, axis=-1, keepdims=True)) * factor
                ).astype(bf16)
            )
            low.append(attention.astype(bf16))
        gq_ref[:, span] = dot(
            jnp.concatenate(slopes, axis=1), jnp.concatenate(split(k_ref[:, span]), axis=0)
        ).astype(bf16)
        gk_ref[:, span] = t_dot(
            jnp.concatenate(slopes, axis=0), jnp.concatenate(split(q_ref[:, span]), axis=0)
        ).astype(bf16)
        gv_ref[:, span] = t_dot(
            jnp.concatenate(low, axis=0), jnp.concatenate(upper, axis=0)
        ).astype(bf16)
    grad_hidden = dot_t(gq_ref[...], query_ref[...])
    grad_hidden = grad_hidden + dot_t(gk_ref[...], key_ref[...])
    grad_hidden = grad_hidden + dot_t(gv_ref[...], value_ref[...])
    grad_tokens = (grad_stream + norm_back(grad_hidden, unit_one, inverse_one, gain_one)).astype(
        bf16
    )
    grad_patches = dot_t(grad_tokens, patch_ref[...]).astype(bf16)
    grad_sorted = dot_t(grad_patches, order_ref[...])
    for p in range(SIDE):
        for j in range(HALF):
            turned_ref[p, pl.ds(j, SIDE, stride=HALF), :] = grad_sorted[
                p * SIDE : (p + 1) * SIDE, j * 128 : (j + 1) * 128
            ]
    for p in range(SIDE):
        lines = turned_ref[p].T
        for color in range(COLORS):
            colors_ref[color, p * HALF : (p + 1) * HALF, :] = lines[
                color * HALF : (color + 1) * HALF
            ]
    nothing = jnp.zeros((1, width), f32)
    for band in range(bands):
        begin, end = band * row_count, (band + 1) * row_count
        grad_ref[band, 0:rows, :] = (
            colors_ref[:, begin:end, :].reshape(rows, width).astype(bf16)
        )
        lines = []
        for inside, at in ((band > 0, begin - 1), (band < bands - 1, end)):
            for color in range(COLORS):
                lines.append(colors_ref[color, at : at + 1, :] if inside else nothing)
            lines += [nothing] * 4
        grad_ref[band, rows:, :] = jnp.concatenate(lines).astype(bf16)


def reward_pass(parts, weight, patch_weight, position_table, gain_one, wq, wk, wv, wo, gain_two, head):
    bands, _, rows, width = parts.shape
    vmem = pl.BlockSpec(memory_space=pltpu.VMEM)
    square = pltpu.VMEM((TOKENS_F, D), bf16)
    return pl.pallas_call(
        reward_kernel,
        out_shape=(
            jax.ShapeDtypeStruct((1, 1), f32),
            jax.ShapeDtypeStruct((bands, rows, width), bf16),
        ),
        in_specs=[vmem] * 12,
        out_specs=(vmem, vmem),
        scratch_shapes=[
            pltpu.VMEM((COLORS, width, width), f32),
            pltpu.VMEM((SIDE, 128, 128), f32),
        ]
        + [square] * 9
        + [pltpu.VMEM((HEADS, TOKENS_F, TOKENS_F), f32)],
        compiler_params=pltpu.CompilerParams(vmem_limit_bytes=VMEM_LIMIT),
        name="reward_pass",
    )(
        parts,
        weight.reshape(1, 1),
        patch_order(),
        patch_weight,
        position_table,
        gain_one.reshape(1, D),
        wq,
        wk,
        wv,
        wo,
        gain_two.reshape(1, D),
        head.reshape(1, D),
    )


def on_device(
    features,
    conv_kernel,
    patch_weight,
    position_table,
    gain_one,
    query_weight,
    key_weight,
    value_weight,
    out_weight,
    gain_two,
    head_vector,
    frame_weight,
):
    clip_count, frame_count, chan_count, row_count, width = features.shape
    band_count = lax.axis_size("sp")
    core_count = lax.axis_size("mdl")
    time_count = lax.axis_size("tm")
    rows = COLORS * row_count + 32
    whole_query, whole_key, whole_value, whole_out = (
        lax.all_gather(matrix, "sp", axis=0, tiled=True)
        for matrix in (query_weight, key_weight, value_weight, out_weight)
    )
    upward = [(i, i + 1) for i in range(time_count - 1)]
    downward = [(i + 1, i) for i in range(time_count - 1)]

    band_forward, band_back = band_matrices(conv_kernel, row_count)
    spilled = partial_colors(features, band_forward)
    from_below = lax.ppermute(spilled[frame_count + 1], "tm", upward)
    from_above = lax.ppermute(spilled[0], "tm", downward)
    sent = spilled[1 : frame_count + 1]
    sent = sent.at[0].add(from_below).at[frame_count - 1].add(from_above)
    sent = sent.reshape(band_count * core_count, rows, width)
    parts = lax.all_to_all(sent, ("sp", "mdl"), split_axis=0, concat_axis=0, tiled=True)
    parts = parts.reshape(band_count, core_count, rows, width)
    reward, grad_bands = reward_pass(
        parts,
        frame_weight,
        patch_weight,
        position_table,
        gain_one,
        whole_query,
        whole_key,
        whole_value,
        whole_out,
        gain_two,
        head_vector,
    )
    copies = jnp.broadcast_to(
        grad_bands[:, None], (band_count, core_count, rows, width)
    ).reshape(band_count * core_count, rows, width)
    returned = lax.all_to_all(copies, ("sp", "mdl"), split_axis=0, concat_axis=0, tiled=True)
    returned = returned.reshape(frame_count, clip_count, rows, width)
    before = lax.ppermute(returned[frame_count - 1], "tm", upward)
    after = lax.ppermute(returned[0], "tm", downward)
    grads = jnp.concatenate([before[None], returned, after[None]])
    feature_grad = color_backward(grads, features, band_back)
    return (reward.reshape(1, 1, 1), feature_grad)


def solution(mesh):
    placed = (
        P("grp", "tm", "mdl", "sp", None),
        P(None, None, None, None, "mdl"),
        P(),
        P(),
        P(),
        P("sp", None),
        P("sp", None),
        P("sp", None),
        P("sp", None),
        P(),
        P(),
        P(("grp", "sp"), "tm", "mdl"),
    )
    return jax.shard_map(
        on_device,
        mesh=mesh,
        in_specs=placed,
        out_specs=(P(("grp", "sp"), "tm", "mdl"), P("grp", "tm", "mdl", "sp", None)),
        check_vma=False,
    )
```

```python
import math

import jax
import jax.numpy as jnp
import numpy as np
from jax import lax
from jax.experimental import pallas as pl
from jax.experimental.pallas import tpu as pltpu
from jax.sharding import PartitionSpec as P

D = 1024
HEADS = 16
HEAD_DIM = 64
PATCH = 16
PIX = 768
IMG = 256
TOKENS_F = 256
COLORS = 12
SIDE = IMG // PATCH
HALF = PATCH // 2
VMEM_LIMIT = 56 * 1024 * 1024

loss_scale = 1024.0
norm_eps = 1e-05
f32 = jnp.float32
bf16 = jnp.bfloat16


def sizes(row_count):
    block = min(16, row_count)
    rimmed = -(-(block + 2) // 8) * 8
    deep = 3 * COLORS * rimmed
    padded = -(-deep // 128) * 128
    return block, row_count // block, rimmed, deep, padded


def band_kernel(block, rimmed, conv_ref, fwd_ref, back_ref, spread_ref, wide_ref):
    chans = conv_ref.shape[-1]
    wide = chans * block
    deep = 3 * COLORS * rimmed
    padded = wide_ref.shape[0]
    lane_chan = lax.broadcasted_iota(jnp.int32, (chans, wide), 1) // block
    own_chan = lax.broadcasted_iota(jnp.int32, (chans, wide), 0)
    repeat = jnp.where(lane_chan == own_chan, 1.0, 0.0).astype(bf16)
    lane_row = lax.broadcasted_iota(jnp.int32, (rimmed, wide), 1) % block
    rim_row = lax.broadcasted_iota(jnp.int32, (rimmed, wide), 0)
    masks = [rim_row == lane_row + (2 - tap) for tap in range(3)]
    for col_tap in range(3):
        for row_tap in range(3):
            spread_ref[row_tap] = jnp.dot(
                conv_ref[row_tap, col_tap], repeat, preferred_element_type=f32
            )

        @pl.loop(0, 3 * COLORS)
        def _(line):
            total = jnp.zeros((rimmed, wide), f32)
            for row_tap in range(3):
                row = spread_ref[row_tap, pl.ds(line, 1), :]
                total = jnp.where(masks[row_tap], jnp.broadcast_to(row, (rimmed, wide)), total)
            wide_ref[pl.ds(pl.multiple_of(line * rimmed, 8), rimmed), :] = total

        if padded > deep:
            wide_ref[deep:, :] = jnp.zeros((padded - deep, wide), f32)
        fwd_ref[:, col_tap * wide : (col_tap + 1) * wide] = wide_ref[...].astype(bf16)
        back_ref[:, col_tap * padded : (col_tap + 1) * padded] = wide_ref[...].T.astype(bf16)


def band_matrices(conv_kernel, row_count):
    block, _, rimmed, deep, padded = sizes(row_count)
    chans = conv_kernel.shape[-1]
    wide = chans * block
    taps = conv_kernel.transpose(1, 2, 0, 3, 4).reshape(3, 3, 3 * COLORS, chans)

    def body(*refs):
        band_kernel(block, rimmed, *refs)

    return pl.pallas_call(
        body,
        out_shape=(
            jax.ShapeDtypeStruct((padded, 3 * wide), bf16),
            jax.ShapeDtypeStruct((wide, 3 * padded), bf16),
        ),
        in_specs=[pl.BlockSpec(memory_space=pltpu.VMEM)],
        out_specs=(pl.BlockSpec(memory_space=pltpu.VMEM), pl.BlockSpec(memory_space=pltpu.VMEM)),
        scratch_shapes=[pltpu.VMEM((3, 3 * COLORS, wide), f32), pltpu.VMEM((padded, wide), f32)],
        compiler_params=pltpu.CompilerParams(vmem_limit_bytes=VMEM_LIMIT),
        name="band_matrices",
    )(taps)


def column_shifts(values):
    width = values.shape[-1]
    lane = lax.broadcasted_iota(jnp.int32, values.shape, values.ndim - 1)
    before = jnp.where(lane == 0, 0.0, pltpu.roll(values, 1, axis=values.ndim - 1))
    after = jnp.where(lane == width - 1, 0.0, pltpu.roll(values, width - 1, axis=values.ndim - 1))
    return before, values, after


def color_kernel(dims, features_ref, band_ref, main_ref, rim_ref, total_ref, cells_ref):
    frame_count, row_count, block, blocks, rimmed, deep = dims
    chans, width = features_ref.shape[2], features_ref.shape[4]
    wide = chans * block
    total_ref[...] = jnp.zeros_like(total_ref)
    for first in range(0, frame_count, 2):
        for band in range(blocks):
            for half in range(2):
                raw = features_ref[0, first + half, :, band * block : (band + 1) * block, :]
                values = raw.astype(f32).reshape(wide, width)
                active = (values / (1.0 + jnp.exp(-values))).astype(bf16).astype(f32)
                for col_tap, shifted in enumerate(column_shifts(active)):
                    cells_ref[
                        col_tap * wide : (col_tap + 1) * wide, half * width : (half + 1) * width
                    ] = shifted.astype(bf16)
            product = jnp.dot(band_ref[...], cells_ref[...], preferred_element_type=f32)
            product = product[:deep].reshape(3, COLORS, rimmed, 2 * width)
            for half in range(2):
                for time_tap in range(3):
                    total_ref[
                        first + half - time_tap + 2, :, band * block : band * block + rimmed, :
                    ] += product[time_tap, :, :, half * width : (half + 1) * width]
    rows = COLORS * row_count
    for frame in range(frame_count + 2):
        part = total_ref[frame]
        if frame == 0:
            into = rim_ref.at[0, 0]
        elif frame == frame_count + 1:
            into = rim_ref.at[1, 0]
        else:
            into = main_ref.at[frame - 1, 0]
        into[0:rows, :] = part[:, 1 : row_count + 1, :].reshape(rows, width).astype(bf16)
        spare = jnp.zeros((4, width), f32)
        top = [part[color, 0:1, :] for color in range(COLORS)]
        low = [part[color, row_count + 1 : row_count + 2, :] for color in range(COLORS)]
        into[rows:, :] = jnp.concatenate(top + [spare] + low + [spare]).astype(bf16)


def partial_colors(features, band):
    clip_count, frame_count, chans, row_count, width = features.shape
    block, blocks, rimmed, deep, padded = sizes(row_count)
    rows = COLORS * row_count + 32
    stored = (blocks - 1) * block + rimmed
    dims = (frame_count, row_count, block, blocks, rimmed, deep)

    def body(*refs):
        color_kernel(dims, *refs)

    return pl.pallas_call(
        body,
        grid=(clip_count,),
        out_shape=(
            jax.ShapeDtypeStruct((frame_count, clip_count, rows, width), bf16),
            jax.ShapeDtypeStruct((2, clip_count, rows, width), bf16),
        ),
        in_specs=[
            pl.BlockSpec((1, frame_count, chans, row_count, width), lambda clip: (clip, 0, 0, 0, 0)),
            pl.BlockSpec(memory_space=pltpu.VMEM),
        ],
        out_specs=(
            pl.BlockSpec((frame_count, 1, rows, width), lambda clip: (0, clip, 0, 0)),
            pl.BlockSpec((2, 1, rows, width), lambda clip: (0, clip, 0, 0)),
        ),
        scratch_shapes=[
            pltpu.VMEM((frame_count + 2, COLORS, stored, width), f32),
            pltpu.VMEM((3 * chans * block, 2 * width), bf16),
        ],
        compiler_params=pltpu.CompilerParams(vmem_limit_bytes=VMEM_LIMIT),
        name="partial_colors",
    )(features, band)


def color_backward_kernel(dims, grad_ref, features_ref, band_ref, out_ref, rim_ref, shift_ref, cells_ref):
    frame_count, row_count, block, blocks, rimmed, deep, padded = dims
    chans, width = features_ref.shape[2], features_ref.shape[4]
    rows = COLORS * row_count
    color_rows = COLORS * rimmed
    stored = rim_ref.shape[1]
    for frame in range(frame_count + 2):
        for color in range(COLORS):
            rim_ref[color, 1 : row_count + 1, :] = grad_ref[
                frame, 0, color * row_count : (color + 1) * row_count, :
            ].astype(f32)
        edges = grad_ref[frame, 0, rows:, :].astype(f32)
        for color in range(COLORS):
            rim_ref[color, 0:1, :] = edges[color : color + 1]
            rim_ref[color, row_count + 1 : row_count + 2, :] = edges[16 + color : 17 + color]
            rim_ref[color, row_count + 2 :, :] = jnp.zeros((stored - row_count - 2, width), f32)
        for band in range(blocks):
            lines = rim_ref[:, band * block : band * block + rimmed, :].reshape(color_rows, width)
            before, same, after = column_shifts(lines)
            for col_tap, shifted in enumerate((after, same, before)):
                shift_ref[col_tap, frame, band] = shifted.astype(bf16)
    if padded > deep:
        for col_tap in range(3):
            cells_ref[col_tap * padded + deep : (col_tap + 1) * padded, :] = jnp.zeros(
                (padded - deep, 2 * width), bf16
            )
    for first in range(0, frame_count, 2):
        for band in range(blocks):
            for half in range(2):
                for col_tap in range(3):
                    for time_tap in range(3):
                        begin = col_tap * padded + time_tap * color_rows
                        cells_ref[
                            begin : begin + color_rows, half * width : (half + 1) * width
                        ] = shift_ref[col_tap, first + half - time_tap + 2, band]
            product = jnp.dot(band_ref[...], cells_ref[...], preferred_element_type=f32)
            for half in range(2):
                values = features_ref[
                    0, first + half, :, band * block : (band + 1) * block, :
                ].astype(f32)
                logistic = 1.0 / (1.0 + jnp.exp(-values))
                slope = logistic * (1.0 + values * (1.0 - logistic))
                grad = product[:, half * width : (half + 1) * width].reshape(chans, block, width)
                out_ref[0, first + half, :, band * block : (band + 1) * block, :] = (
                    grad * slope
                ).astype(bf16)


def color_backward(grads, features, band):
    clip_count, frame_count, chans, row_count, width = features.shape
    block, blocks, rimmed, deep, padded = sizes(row_count)
    rows = COLORS * row_count + 32
    stored = (blocks - 1) * block + rimmed
    dims = (frame_count, row_count, block, blocks, rimmed, deep, padded)
    whole = pl.BlockSpec((1, frame_count, chans, row_count, width), lambda clip: (clip, 0, 0, 0, 0))

    def body(*refs):
        color_backward_kernel(dims, *refs)

    return pl.pallas_call(
        body,
        grid=(clip_count,),
        out_shape=jax.ShapeDtypeStruct(features.shape, bf16),
        in_specs=[
            pl.BlockSpec((frame_count + 2, 1, rows, width), lambda clip: (0, clip, 0, 0)),
            whole,
            pl.BlockSpec(memory_space=pltpu.VMEM),
        ],
        out_specs=whole,
        scratch_shapes=[
            pltpu.VMEM((COLORS, stored, width), f32),
            pltpu.VMEM((3, frame_count + 2, blocks, COLORS * rimmed, width), bf16),
            pltpu.VMEM((3 * padded, 2 * width), bf16),
        ],
        compiler_params=pltpu.CompilerParams(vmem_limit_bytes=VMEM_LIMIT),
        name="color_backward",
    )(grads, features, band)


def patch_order():
    table = np.zeros((HALF, 128, PIX), np.float32)
    for color in range(COLORS):
        k, a, b = color // 4, (color // 2) % 2, color % 2
        for i in range(HALF):
            for j in range(HALF):
                table[j, color * HALF + i, k * PATCH * PATCH + (2 * i + a) * PATCH + 2 * j + b] = 1
    return jnp.asarray(table.reshape(HALF * 128, PIX), bf16)


def layer_norm(values, gain):
    center = values - jnp.mean(values, axis=-1, keepdims=True)
    inverse = lax.rsqrt(jnp.mean(center * center, axis=-1, keepdims=True) + norm_eps)
    normed = center * inverse
    return (normed * gain, normed, inverse)


def norm_back(upstream, normed, inverse, gain):
    scaled = upstream * gain
    return inverse * (
        scaled
        - jnp.mean(scaled, axis=-1, keepdims=True)
        - normed * jnp.mean(scaled * normed, axis=-1, keepdims=True)
    )


def dot(left, right):
    return jnp.dot(left, right, preferred_element_type=f32)


def dot_t(left, right):
    return lax.dot_general(left, right, (((1,), (1,)), ((), ())), preferred_element_type=f32)


def t_dot(left, right):
    return lax.dot_general(left, right, (((0,), (0,)), ((), ())), preferred_element_type=f32)


def reward_kernel(
    parts_ref,
    weight_ref,
    order_ref,
    patch_ref,
    position_ref,
    gain_one_ref,
    whole_ref,
    gain_two_ref,
    head_ref,
    reward_ref,
    grad_ref,
    colors_ref,
    turned_ref,
    tokens_ref,
    q_ref,
    k_ref,
    v_ref,
    gm_ref,
    mix_ref,
    gq_ref,
    gk_ref,
    gv_ref,
    att_ref,
):
    query_ref, key_ref, value_ref, out_ref = (
        whole_ref.at[:, i * D : (i + 1) * D] for i in range(4)
    )
    bands, cores = parts_ref.shape[0], parts_ref.shape[1]
    width = parts_ref.shape[-1]
    row_count = width // bands
    rows = COLORS * row_count
    edges = []
    for band in range(bands):
        part = parts_ref[band, 0].astype(f32)
        for core in range(1, cores):
            part = part + parts_ref[band, core].astype(f32)
        for color in range(COLORS):
            colors_ref[color, band * row_count : (band + 1) * row_count, :] = part[
                color * row_count : (color + 1) * row_count
            ]
        edges.append(part[rows:])
    for band in range(bands):
        for color in range(COLORS):
            if band > 0:
                at = band * row_count - 1
                colors_ref[color, at : at + 1, :] += edges[band][color : color + 1]
            if band < bands - 1:
                at = (band + 1) * row_count
                colors_ref[color, at : at + 1, :] += edges[band][16 + color : 17 + color]
    spare = jnp.zeros((128 - COLORS * HALF, width), f32)
    for p in range(SIDE):
        lines = [colors_ref[color, p * HALF : (p + 1) * HALF, :] for color in range(COLORS)]
        turned_ref[p] = jnp.concatenate(lines + [spare]).T
    for p in range(SIDE):
        for j in range(HALF):
            tokens_ref[p * SIDE : (p + 1) * SIDE, j * 128 : (j + 1) * 128] = turned_ref[
                p, pl.ds(j, SIDE, stride=HALF), :
            ].astype(bf16)
    patches = dot(tokens_ref[...], order_ref[...]).astype(bf16)
    tokens = (dot(patches, patch_ref[...]) + position_ref[...].astype(f32)).astype(bf16)
    gain_one = gain_one_ref[...]
    gain_two = gain_two_ref[...]
    head = head_ref[...]
    normed_one, unit_one, inverse_one = layer_norm(tokens.astype(f32), gain_one)
    hidden = normed_one.astype(bf16)
    q_ref[...] = dot(hidden, query_ref[...]).astype(bf16)
    k_ref[...] = dot(hidden, key_ref[...]).astype(bf16)
    v_ref[...] = dot(hidden, value_ref[...]).astype(bf16)
    factor = 1.0 / math.sqrt(HEAD_DIM)
    pair_width = 2 * HEAD_DIM
    side = lax.broadcasted_iota(jnp.int32, (TOKENS_F, pair_width), 1) // HEAD_DIM
    zero = jnp.zeros((TOKENS_F, pair_width), bf16)

    def split(values):
        return [jnp.where(side == half, values, zero) for half in range(2)]

    for pair in range(HEADS // 2):
        span = slice(pair * pair_width, (pair + 1) * pair_width)
        queries = split(q_ref[:, span])
        keys = k_ref[:, span]
        low = []
        for half in range(2):
            scores = dot_t(queries[half], keys) * factor
            powers = jnp.exp(scores - jnp.max(scores, axis=-1, keepdims=True))
            attention = powers * (1.0 / jnp.sum(powers, axis=-1, keepdims=True))
            att_ref[2 * pair + half] = attention
            low.append(attention.astype(bf16))
        values = split(v_ref[:, span])
        mix_ref[:, span] = dot(
            jnp.concatenate(low, axis=1), jnp.concatenate(values, axis=0)
        ).astype(bf16)
    stream = tokens.astype(f32) + dot(mix_ref[...], out_ref[...])
    normed_two, unit_two, inverse_two = layer_norm(stream, gain_two)
    reward_ref[...] = (
        jnp.sum(jnp.sum(normed_two * head, axis=0, keepdims=True), axis=1, keepdims=True) / TOKENS_F
    )
    upstream = head * (loss_scale * weight_ref[...] / TOKENS_F)
    grad_stream = norm_back(upstream, unit_two, inverse_two, gain_two)
    gm_ref[...] = dot_t(grad_stream.astype(bf16), out_ref[...]).astype(bf16)
    for pair in range(HEADS // 2):
        span = slice(pair * pair_width, (pair + 1) * pair_width)
        upper = split(gm_ref[:, span])
        values = v_ref[:, span]
        slopes, low = [], []
        for half in range(2):
            attention = att_ref[2 * pair + half]
            grad_attention = dot_t(upper[half], values)
            weighted = attention * grad_attention
            slopes.append(
                (
                    (weighted - attention * jnp.sum(weighted, axis=-1, keepdims=True)) * factor
                ).astype(bf16)
            )
            low.append(attention.astype(bf16))
        gq_ref[:, span] = dot(
            jnp.concatenate(slopes, axis=1), jnp.concatenate(split(k_ref[:, span]), axis=0)
        ).astype(bf16)
        gk_ref[:, span] = t_dot(
            jnp.concatenate(slopes, axis=0), jnp.concatenate(split(q_ref[:, span]), axis=0)
        ).astype(bf16)
        gv_ref[:, span] = t_dot(
            jnp.concatenate(low, axis=0), jnp.concatenate(upper, axis=0)
        ).astype(bf16)
    grad_hidden = dot_t(gq_ref[...], query_ref[...])
    grad_hidden = grad_hidden + dot_t(gk_ref[...], key_ref[...])
    grad_hidden = grad_hidden + dot_t(gv_ref[...], value_ref[...])
    grad_tokens = (grad_stream + norm_back(grad_hidden, unit_one, inverse_one, gain_one)).astype(
        bf16
    )
    grad_patches = dot_t(grad_tokens, patch_ref[...]).astype(bf16)
    grad_sorted = dot_t(grad_patches, order_ref[...])
    for p in range(SIDE):
        for j in range(HALF):
            turned_ref[p, pl.ds(j, SIDE, stride=HALF), :] = grad_sorted[
                p * SIDE : (p + 1) * SIDE, j * 128 : (j + 1) * 128
            ]
    for p in range(SIDE):
        lines = turned_ref[p].T
        for color in range(COLORS):
            colors_ref[color, p * HALF : (p + 1) * HALF, :] = lines[
                color * HALF : (color + 1) * HALF
            ]
    nothing = jnp.zeros((1, width), f32)
    for band in range(bands):
        begin, end = band * row_count, (band + 1) * row_count
        grad_ref[band, 0:rows, :] = (
            colors_ref[:, begin:end, :].reshape(rows, width).astype(bf16)
        )
        lines = []
        for inside, at in ((band > 0, begin - 1), (band < bands - 1, end)):
            for color in range(COLORS):
                lines.append(colors_ref[color, at : at + 1, :] if inside else nothing)
            lines += [nothing] * 4
        grad_ref[band, rows:, :] = jnp.concatenate(lines).astype(bf16)


def reward_pass(parts, weight, patch_weight, position_table, gain_one, whole, gain_two, head):
    bands, _, rows, width = parts.shape
    vmem = pl.BlockSpec(memory_space=pltpu.VMEM)
    square = pltpu.VMEM((TOKENS_F, D), bf16)
    return pl.pallas_call(
        reward_kernel,
        out_shape=(
            jax.ShapeDtypeStruct((1, 1), f32),
            jax.ShapeDtypeStruct((bands, rows, width), bf16),
        ),
        in_specs=[vmem] * 9,
        out_specs=(vmem, vmem),
        scratch_shapes=[
            pltpu.VMEM((COLORS, width, width), f32),
            pltpu.VMEM((SIDE, 128, 128), f32),
        ]
        + [square] * 9
        + [pltpu.VMEM((HEADS, TOKENS_F, TOKENS_F), f32)],
        compiler_params=pltpu.CompilerParams(vmem_limit_bytes=VMEM_LIMIT),
        name="reward_pass",
    )(
        parts,
        weight.reshape(1, 1),
        patch_order(),
        patch_weight,
        position_table,
        gain_one.reshape(1, D),
        whole,
        gain_two.reshape(1, D),
        head.reshape(1, D),
    )


def meet(time, times, band, bands, core):
    barrier = pltpu.get_barrier_semaphore()

    def greet(where):
        pl.semaphore_signal(barrier, inc=1, device_id=where, device_id_type=pl.DeviceIdType.MESH)

    greet({"mdl": 1 - core})
    for step in range(1, bands):
        greet({"sp": lax.rem(band + step, bands)})
    count = bands
    for inside, there in ((time > 0, time - 1), (time < times - 1, time + 1)):

        @pl.when(inside)
        def _():
            for other in range(2):
                greet({"tm": there, "mdl": other})

        count = count + 2 * inside.astype(jnp.int32)
    pl.semaphore_wait(barrier, count)


def remote(source, target, send_sem, recv_sem, where):
    return pltpu.make_async_remote_copy(
        src_ref=source,
        dst_ref=target,
        send_sem=send_sem,
        recv_sem=recv_sem,
        device_id=where,
        device_id_type=pl.DeviceIdType.MESH,
    )


def gather_colors_kernel(
    dims,
    main_ref,
    rim_ref,
    out_ref,
    core_ref,
    time_ref,
    ready_ref,
    band_ref,
    core_sems,
    time_send,
    time_recv,
    band_send,
    band_recv,
):
    bands, times, clips, last = dims
    time, band, core = lax.axis_index("tm"), lax.axis_index("sp"), lax.axis_index("mdl")
    meet(time, times, band, bands, core)
    to_core = remote(
        main_ref.at[:, 1 - core], core_ref, core_sems.at[0], core_sems.at[1], {"mdl": 1 - core}
    )
    to_core.start()
    rims = []
    for clip in range(clips):
        rims.append((0, clip, last + clip, time > 0, time - 1, time < times - 1))
        rims.append((1, clip, clip, time < times - 1, time + 1, time > 0))

    def rim_copy(side, clip, place, there):
        return remote(
            rim_ref.at[side, clip],
            time_ref.at[side, core, clip],
            time_send.at[side, clip],
            time_recv.at[side, core, clip],
            {"tm": there, "mdl": place % 2},
        )

    for side, clip, place, sends, there, _ in rims:

        @pl.when(sends)
        def _():
            rim_copy(side, clip, place, there).start()

    for side, clip, place, _, there, receives in rims:

        @pl.when(jnp.logical_and(receives, core == place % 2))
        def _():
            for other in range(2):
                remote(
                    rim_ref.at[side, clip],
                    time_ref.at[side, other, clip],
                    time_send.at[side, clip],
                    time_recv.at[side, other, clip],
                    {"mdl": 1 - core},
                ).wait_recv()

    to_core.wait_recv()

    def band_copy(step, target, source):
        return remote(
            ready_ref.at[target],
            band_ref.at[source],
            band_send.at[step],
            band_recv.at[source],
            {"sp": target},
        )

    for step in list(range(1, bands)) + [0]:
        target = lax.rem(band + step, bands)
        total = main_ref[target, core].astype(f32) + core_ref[target].astype(f32)
        ready_ref[target] = total.astype(bf16)
        for side, clip, place, _, _, receives in rims:
            here = jnp.logical_and(target == place // 2, core == place % 2)

            @pl.when(jnp.logical_and(receives, here))
            def _():
                more = main_ref[target, core].astype(f32) + core_ref[target].astype(f32)
                for other in range(2):
                    more = more + time_ref[side, other, clip].astype(f32)
                ready_ref[target] = more.astype(bf16)

        if step:
            band_copy(step, target, band).start()
    out_ref[band, 0] = ready_ref[band]
    for step in range(1, bands):
        source = lax.rem(band - step + bands, bands)
        remote(
            ready_ref.at[source],
            band_ref.at[source],
            band_send.at[step],
            band_recv.at[source],
            {"sp": source},
        ).wait_recv()
        out_ref[source, 0] = band_ref[source]
    to_core.wait_send()
    for step in range(1, bands):
        band_copy(step, lax.rem(band + step, bands), band).wait_send()
    for side, clip, place, sends, there, _ in rims:

        @pl.when(sends)
        def _():
            rim_copy(side, clip, place, there).wait_send()


def gather_colors(main, rim, bands, times):
    frame_count, clips, rows, width = main.shape
    main = main.reshape(bands, 2, rows, width)
    dims = (bands, times, clips, (frame_count - 1) * clips)
    vmem = pl.BlockSpec(memory_space=pltpu.VMEM)

    def body(*refs):
        gather_colors_kernel(dims, *refs)

    return pl.pallas_call(
        body,
        out_shape=jax.ShapeDtypeStruct((bands, 1, rows, width), bf16),
        in_specs=[vmem, vmem],
        out_specs=vmem,
        scratch_shapes=[
            pltpu.VMEM((bands, rows, width), bf16),
            pltpu.VMEM((2, 2, clips, rows, width), bf16),
            pltpu.VMEM((bands, rows, width), bf16),
            pltpu.VMEM((bands, rows, width), bf16),
            pltpu.SemaphoreType.DMA((2,)),
            pltpu.SemaphoreType.DMA((2, clips)),
            pltpu.SemaphoreType.DMA((2, 2, clips)),
            pltpu.SemaphoreType.DMA((bands,)),
            pltpu.SemaphoreType.DMA((bands,)),
        ],
        compiler_params=pltpu.CompilerParams(
            vmem_limit_bytes=VMEM_LIMIT, collective_id=1, has_side_effects=True
        ),
        name="gather_colors",
    )(main, rim)


def scatter_grads_kernel(
    dims,
    grad_ref,
    out_ref,
    land_ref,
    band_send,
    band_recv,
    core_send,
    core_recv,
    time_send,
    time_recv,
):
    bands, times, clips, places = dims
    time, band, core = lax.axis_index("tm"), lax.axis_index("sp"), lax.axis_index("mdl")
    meet(time, times, band, bands, core)

    def band_copy(step, target, source):
        return remote(
            grad_ref.at[target],
            land_ref.at[clips + source * 2 + core],
            band_send.at[step],
            band_recv.at[source],
            {"sp": target},
        )

    for step in range(1, bands):
        band_copy(step, lax.rem(band + step, bands), band).start()
    rims = []
    for clip in range(clips):
        rims.append((0, clip, clip, clips + places + clip, time > 0, time - 1, time < times - 1))
        rims.append((1, clip, places - clips + clip, clip, time < times - 1, time + 1, time > 0))

    def core_copy(block, source, side):
        return remote(
            block,
            land_ref.at[clips + source * 2 + side],
            core_send.at[source],
            core_recv.at[source],
            {"mdl": 1 - core},
        )

    def rim_copy(block, rim, other):
        side, clip, _, slot, _, there, _ = rim
        return remote(
            block,
            land_ref.at[slot],
            time_send.at[side, clip, other],
            time_recv.at[side, clip],
            {"tm": there, "mdl": other},
        )

    def pass_on(block, source):
        core_copy(block, source, core).start()
        for rim in rims:
            here = jnp.logical_and(source == rim[2] // 2, core == rim[2] % 2)

            @pl.when(jnp.logical_and(rim[4], here))
            def _():
                for other in range(2):
                    rim_copy(block, rim, other).start()

    pass_on(grad_ref.at[band], band)
    out_ref[clips + band * 2 + core] = grad_ref[band]
    for step in range(1, bands):
        source = lax.rem(band - step + bands, bands)
        band_copy(step, source, source).wait_recv()
        pass_on(land_ref.at[clips + source * 2 + core], source)
        out_ref[clips + source * 2 + core] = land_ref[clips + source * 2 + core]
    for step in range(bands):
        source = lax.rem(band - step + bands, bands)
        core_copy(grad_ref.at[band], source, 1 - core).wait_recv()
        out_ref[clips + source * 2 + 1 - core] = land_ref[clips + source * 2 + 1 - core]
    for rim in rims:

        @pl.when(rim[6])
        def _():
            remote(
                grad_ref.at[band],
                land_ref.at[rim[3]],
                time_send.at[rim[0], rim[1], 0],
                time_recv.at[rim[0], rim[1]],
                {"mdl": 1 - core},
            ).wait_recv()
            out_ref[rim[3]] = land_ref[rim[3]]

        @pl.when(jnp.logical_not(rim[6]))
        def _():
            out_ref[rim[3]] = jnp.zeros(out_ref.shape[1:], bf16)

    for step in range(1, bands):
        band_copy(step, lax.rem(band + step, bands), band).wait_send()
    for step in range(bands):
        source = lax.rem(band - step + bands, bands)
        core_copy(grad_ref.at[band], source, core).wait_send()
    for rim in rims:

        @pl.when(jnp.logical_and(rim[4], core == rim[2] % 2))
        def _():
            for other in range(2):
                rim_copy(grad_ref.at[band], rim, other).wait_send()


def scatter_grads(grads, frame_count, clips, times):
    bands, rows, width = grads.shape
    places = frame_count * clips
    dims = (bands, times, clips, places)
    slots = places + 2 * clips
    vmem = pl.BlockSpec(memory_space=pltpu.VMEM)

    def body(*refs):
        scatter_grads_kernel(dims, *refs)

    out = pl.pallas_call(
        body,
        out_shape=jax.ShapeDtypeStruct((slots, rows, width), bf16),
        in_specs=[vmem],
        out_specs=vmem,
        scratch_shapes=[
            pltpu.VMEM((slots, rows, width), bf16),
            pltpu.SemaphoreType.DMA((bands,)),
            pltpu.SemaphoreType.DMA((bands,)),
            pltpu.SemaphoreType.DMA((bands,)),
            pltpu.SemaphoreType.DMA((bands,)),
            pltpu.SemaphoreType.DMA((2, clips, 2)),
            pltpu.SemaphoreType.DMA((2, clips)),
        ],
        compiler_params=pltpu.CompilerParams(
            vmem_limit_bytes=VMEM_LIMIT, collective_id=2, has_side_effects=True
        ),
        name="scatter_grads",
    )(grads)
    return out.reshape(frame_count + 2, clips, rows, width)


def on_device(
    features,
    conv_kernel,
    patch_weight,
    position_table,
    gain_one,
    query_weight,
    key_weight,
    value_weight,
    out_weight,
    gain_two,
    head_vector,
    frame_weight,
):
    clip_count, frame_count, chan_count, row_count, width = features.shape
    band_count = lax.axis_size("sp")
    time_count = lax.axis_size("tm")
    holders = ("grp", "tm", "mdl")
    share = query_weight.shape[0] // lax.axis_size(holders)
    begin = lax.axis_index(holders) * share
    stack = jnp.concatenate(
        [
            lax.dynamic_slice_in_dim(matrix, begin, share, axis=0)
            for matrix in (query_weight, key_weight, value_weight, out_weight)
        ],
        axis=1,
    )
    whole = lax.all_gather(stack, ("sp",) + holders, axis=0, tiled=True)
    band_forward, band_back = band_matrices(conv_kernel, row_count)
    main, rim = partial_colors(features, band_forward)
    parts = gather_colors(main, rim, band_count, time_count)
    reward, grad_bands = reward_pass(
        parts,
        frame_weight,
        patch_weight,
        position_table,
        gain_one,
        whole,
        gain_two,
        head_vector,
    )
    grads = scatter_grads(grad_bands, frame_count, clip_count, time_count)
    feature_grad = color_backward(grads, features, band_back)
    return (reward.reshape(1, 1, 1), feature_grad)


def solution(mesh):
    placed = (
        P("grp", "tm", "mdl", "sp", None),
        P(None, None, None, None, "mdl"),
        P(),
        P(),
        P(),
        P("sp", None),
        P("sp", None),
        P("sp", None),
        P("sp", None),
        P(),
        P(),
        P(("grp", "sp"), "tm", "mdl"),
    )
    return jax.shard_map(
        on_device,
        mesh=mesh,
        in_specs=placed,
        out_specs=(P(("grp", "sp"), "tm", "mdl"), P("grp", "tm", "mdl", "sp", None)),
        check_vma=False,
    )
```
